32 devices in a mesh: groups: 2 (over y), row: 4 (over z), col: 4 (over x, core).
Axes of the slice: x: 2, y: 2, z: 4, core: 2. Of those that a mesh axis runs over, the one named last changes fastest.
Arguments:
- integrals: float32 [32, 16, 512], P('groups', ('row', 'col')), parts along dimension 0, may hold values from -6 to 6
- occupied: float32 [32, 16], P('groups'), parts along dimension 0, may hold values from -1.5 to 1.5
- virtual: float32 [32, 16], P('groups'), parts along dimension 0, may hold values from -1.5 to 1.5
- int_mask: int32 [8, 16, 8], P('groups', ('row', 'col')), parts along dimension 0, may hold values 0 or 1
- occ_mask: int32 [8, 4], P('groups'), parts along dimension 0, may hold values 0 or 1
- virt_mask: int32 [8, 4], P('groups'), parts along dimension 0, may hold values 0 or 1
Outputs:
- polarizability: float32 [1024, 512], P(('groups', 'row')), parts along dimension 0
The draws below stay inside these ranges and needn't reach their ends.
There are 2 independent parts, one for each index of `groups`. The reference program is written for one: setup_inputs(seed, part) draws one part's arguments, and reference() takes and returns one part's arrays. A program takes and returns all parts, laid end to end along the dimension named above; each array names one. Nothing has to cross between parts.
All inputs are finite; a program needn't handle non-finite values. No bound on the sum of `int_mask` on one device may be relied on, other than what follows from the above.
Results may differ from the reference program's by a relative error of at most 0.0001.
Values sent between devices are 32-bit elements; how exact they have to be, the bound alone decides.
No kernel may reach another device: no remote copies, remote signals or barrier semaphores. Data moves between devices by JAX's collectives and lax.ppermute only.
A program may use at most 64 MiB of HBM per device.

```python
import jax
import jax.numpy as jnp
from jax import lax

NAUX = 512
ATILE = 64
NB = 16
GTILE = 4


def touch_ends(values, stream_key, smallest, largest):
    shape = values.shape
    spot = [jax.random.randint(jax.random.fold_in(stream_key, axis), (), 0, shape[axis]) for axis in range(len(shape))]
    values = values.at[tuple(spot)].set(smallest)
    longest = shape.index(max(shape))
    spot[longest] = (spot[longest] + 1) % shape[longest]
    return values.at[tuple(spot)].set(largest)


def shard_levels(key, extent, pieces, low, top_value):
    def one(dim, blocks):
        steps = jax.random.uniform(jax.random.fold_in(jax.random.fold_in(key, 6), dim), (blocks,), jnp.float32, low / len(pieces), top_value / len(pieces))
        return jnp.repeat(jnp.exp(steps), extent[dim] // blocks).reshape((-1,) + (1,) * (len(extent) - dim - 1))

    loudness = one(*pieces[0])
    for cut in pieces[1:]:
        loudness = loudness * one(*cut)
    return loudness


def bell_draw(stream_key, dims, scale, limit, cuts=(), held_as=jnp.bfloat16):
    factor_of = shard_levels(stream_key, dims, cuts, -0.22, 0.18) if cuts else 1.0
    entries = jax.random.normal(stream_key, dims, jnp.float32) * scale * factor_of
    return jnp.minimum(jnp.maximum(entries, -limit), limit).astype(held_as)


def setup_inputs(seed: int = 0, part: int = 0) -> dict:
    arg_keys = jax.random.split(jax.random.key(seed), 7)
    own_keys = jax.random.split(jax.random.fold_in(arg_keys[6], part), 7)
    integrals = bell_draw(own_keys[0], (NB, NB, NAUX), 1.0, 6.0, ((1, 16),), jnp.float32)
    occupied = bell_draw(own_keys[1], (NB, NB), NB ** -0.5, 1.5, (), jnp.float32)
    virtual = bell_draw(own_keys[2], (NB, NB), NB ** -0.5, 1.5, (), jnp.float32)
    int_mask = touch_ends((jax.random.randint(own_keys[3], (NB // GTILE, NB, NAUX // ATILE), 0, 4) < 3).astype(jnp.int32), jax.random.fold_in(own_keys[3], 1), 0, 1)
    occ_mask = touch_ends((jax.random.randint(own_keys[4], (NB // GTILE, NB // GTILE), 0, 3) < 2).astype(jnp.int32), jax.random.fold_in(own_keys[4], 1), 0, 1)
    virt_mask = touch_ends((jax.random.randint(own_keys[5], (NB // GTILE, NB // GTILE), 0, 3) < 2).astype(jnp.int32), jax.random.fold_in(own_keys[5], 1), 0, 1)
    return dict(integrals=integrals, occupied=occupied, virtual=virtual, int_mask=int_mask, occ_mask=occ_mask, virt_mask=virt_mask)


def spread_two(mask, tile_rows, tile_cols):
    outer, inner = mask.shape
    wide = jnp.broadcast_to(mask[:, None, :, None], (outer, tile_rows, inner, tile_cols))
    return wide.reshape(outer * tile_rows, inner * tile_cols).astype(jnp.float32)


def spread_three(mask, tile_rows, tile_cols):
    outer, middle, inner = mask.shape
    wide = jnp.broadcast_to(mask[:, None, :, :, None], (outer, tile_rows, middle, inner, tile_cols))
    return wide.reshape(outer * tile_rows, middle, inner * tile_cols).astype(jnp.float32)


def reference(integrals, occupied, virtual, int_mask, occ_mask, virt_mask):
    highest = lax.Precision.HIGHEST
    int_full = integrals * spread_three(int_mask, GTILE, ATILE)
    occ_full = occupied * spread_two(occ_mask, GTILE, GTILE)
    virt_full = virtual * spread_two(virt_mask, GTILE, GTILE)
    blocks = NB // GTILE

    def step(index, total):
        start = (index * GTILE).astype(jnp.int32)
        piece = lax.dynamic_slice_in_dim(int_full, start, GTILE, 1)
        occ_part = jnp.einsum("mn,mlp->nlp", occ_full, piece, precision=highest)
        virt_cols = lax.dynamic_slice_in_dim(virt_full, start, GTILE, 1)
        virt_part = jnp.einsum("sl,snq->nlq", virt_cols, int_full, precision=highest)
        return total + jnp.einsum("nlp,nlq->pq", occ_part, virt_part, precision=highest)

    total = lax.fori_loop(0, blocks, step, jnp.zeros((NAUX, NAUX), jnp.float32))
    return total / NB
```

```python
import functools

import jax
import jax.numpy as jnp
from jax import lax
from jax.experimental import pallas as pl
from jax.experimental.pallas import tpu as pltpu
from jax.sharding import PartitionSpec as P

HIGHEST = lax.Precision.HIGHEST


def spread_two(mask, tile_rows, tile_cols):
    outer, inner = mask.shape
    wide = jnp.broadcast_to(mask[:, None, :, None], (outer, tile_rows, inner, tile_cols))
    return wide.reshape(outer * tile_rows, inner * tile_cols).astype(jnp.float32)


def spread_three(mask, tile_rows, tile_cols):
    outer, middle, inner = mask.shape
    wide = jnp.broadcast_to(mask[:, None, :, :, None], (outer, tile_rows, middle, inner, tile_cols))
    return wide.reshape(outer * tile_rows, middle, inner * tile_cols).astype(jnp.float32)


def by_reduction(integrals, occupied, virtual, int_mask, occ_mask, virt_mask):
    basis = occupied.shape[0]
    local_pairs = integrals.shape[1]
    aux_count = integrals.shape[2]
    green_tile = basis // occ_mask.shape[0]
    aux_tile = aux_count // int_mask.shape[2]
    row_count = lax.axis_size("row")
    col_count = lax.axis_size("col")
    int_full = integrals * spread_three(int_mask, green_tile, aux_tile)
    occ_full = occupied * spread_two(occ_mask, green_tile, green_tile)
    virt_full = virtual * spread_two(virt_mask, green_tile, green_tile)
    flat = int_full.reshape(basis, local_pairs * aux_count)
    contract_first = (((0,), (0,)), ((), ()))
    trans_virt = lax.dot_general(
        virt_full, flat, contract_first, precision=HIGHEST, preferred_element_type=jnp.float32
    )
    shaped_virt = trans_virt.reshape(row_count, col_count, local_pairs, local_pairs, aux_count)
    mirrored = lax.all_to_all(
        lax.all_to_all(shaped_virt, "row", split_axis=0, concat_axis=0, tiled=True),
        "col",
        split_axis=1,
        concat_axis=1,
        tiled=True,
    )
    trans_occ = lax.dot_general(
        occ_full, flat, contract_first, precision=HIGHEST, preferred_element_type=jnp.float32
    )
    shaped_occ = trans_occ.reshape(row_count, col_count, local_pairs, local_pairs, aux_count)
    pair_dims = (((0, 1, 2, 3), (0, 1, 3, 2)), ((), ()))
    whole = (
        lax.dot_general(
            shaped_occ, mirrored, pair_dims, precision=HIGHEST, preferred_element_type=jnp.float32
        )
        / basis
    )
    summed = lax.psum(whole, "col")
    return lax.psum_scatter(summed, "row", scatter_dimension=0, tiled=True)


def iota(shape, dim):
    return lax.broadcasted_iota(jnp.int32, shape, dim)


def one_hot(rows, cols, row_tile, col_tile):
    return (iota((rows, cols), 0) // row_tile == iota((rows, cols), 1) // col_tile).astype(jnp.float32)


def repeat_rows(mask, tile):
    rows = [jnp.broadcast_to(mask[i : i + 1], (tile, mask.shape[1])) for i in range(mask.shape[0])]
    return jnp.concatenate(rows, 0)


def dot(a, b, dims=((1,), (0,)), precision=HIGHEST):
    return lax.dot_general(a, b, (dims, ((), ())), precision=precision, preferred_element_type=jnp.float32)


def masking_kernel(integrals, mask, out):
    basis, _, aux = integrals.shape
    tiles = mask.shape[2]
    narrow = repeat_rows(mask[:, 0, :].astype(jnp.float32), basis // mask.shape[0])
    wide = dot(narrow, one_hot(tiles, aux, 1, aux // tiles))
    out[...] = integrals[:, 0, :] * wide


def split(x):
    high = x.astype(jnp.bfloat16)
    return high, (x - high.astype(jnp.float32)).astype(jnp.bfloat16)


def mixing_kernel(order, owner, occupied, virtual, occ_mask, virt_mask, high, low):
    basis = occupied.shape[0]
    tile = basis // occ_mask.shape[0]
    me, lane = owner[0], owner[1]
    picked = jnp.zeros((basis, basis), jnp.int32)
    column = iota((basis, basis), 1)
    for j in range(basis):
        lam = me ^ jnp.where(lane == 1, order[1][j], order[0][j])
        picked = jnp.where(column == j, lam, picked)
    pick = (iota((basis, basis), 0) == picked).astype(jnp.float32)
    wide = one_hot(basis // tile, basis, 1, tile)
    occ_full = occupied[...] * dot(repeat_rows(occ_mask[...].astype(jnp.float32), tile), wide)
    virt_full = virtual[...] * dot(repeat_rows(virt_mask[...].astype(jnp.float32), tile), wide)
    occ_cols = dot(occ_full, pick)
    virt_rows = dot(pick, virt_full, ((0,), (1,)))
    pairs = basis * basis
    occ_wide = dot(occ_cols, one_hot(basis, pairs, 1, basis)) * (1.0 / basis)
    cycle = (iota((basis, pairs), 0) == lax.rem(iota((basis, pairs), 1), basis)).astype(jnp.float32)
    virt_wide = dot(virt_rows, cycle)
    for j in range(basis):
        mix = occ_wide * virt_wide[j : j + 1]
        high[j * basis : (j + 1) * basis, :], low[j * basis : (j + 1) * basis, :] = split(mix)


def product_kernel(count, *refs):
    row, high, low = refs[:3]
    blocks, out = refs[3 : 3 + count], refs[3 + count]
    rows = out.shape[0]
    whole = jnp.concatenate([b[...] for b in blocks], 0)
    g_high, g_low = split(whole)
    mixed = (
        dot(high[...], g_high, precision=None)
        + (dot(high[...], g_low, precision=None) + dot(low[...], g_high, precision=None))
    )
    m_high, m_low = split(mixed)
    start = pl.multiple_of(row[0] * rows, 128)
    at = 0
    parts = []
    for b in blocks:
        parts.append(b[:, pl.ds(start, rows)])
    own_high, own_low = split(jnp.concatenate(parts, 0))
    first = ((0,), (0,))
    out[...] = (
        dot(own_high, m_high, first, None)
        + (dot(own_high, m_low, first, None) + dot(own_low, m_high, first, None))
    )


VMEM = pl.BlockSpec(memory_space=pltpu.VMEM)
SMEM = pl.BlockSpec(memory_space=pltpu.SMEM)


def by_gathering(integrals, occupied, virtual, int_mask, occ_mask, virt_mask):
    basis, _, aux = integrals.shape
    axes = ("row", "col")
    rows = lax.axis_size("row")
    devices = rows * lax.axis_size("col")
    units = devices // 2
    me = lax.axis_index("row") * lax.axis_size("col") + lax.axis_index("col")
    lane = me % 2

    def exchange(block, odd, even):
        return lax.ppermute(block, axes, [(i, i ^ (odd if i % 2 else even)) for i in range(devices)])

    half = units // 2
    first = half + 1
    far = [k for k in range(half, units) if k != first]
    steps = list(zip(far, range(1, half)))

    mine = pl.pallas_call(
        masking_kernel,
        out_shape=jax.ShapeDtypeStruct((basis, aux), jnp.float32),
        in_specs=[VMEM, VMEM],
        out_specs=VMEM,
    )(integrals, int_mask)
    mate = exchange(mine, 1, 1)
    got = [exchange(mine, 2 * first, 2 * first)]
    both = jnp.concatenate([mine, mate], 0)
    got += [exchange(both, 2 * odd, 2 * even) for odd, even in steps]
    cut = (len(got) + 1) // 2
    early = exchange(jnp.concatenate(got[:cut], 0), 1, 1)
    late_given = jnp.concatenate(got[cut:], 0)
    late = exchange(late_given, 1, 1)

    order = []
    for this in (0, 1):
        reached = [[2 * first]]
        for pair in steps:
            reached.append([2 * pair[1 - this], 2 * pair[1 - this] + 1])
        other = [[2 * first + 1]]
        for pair in steps:
            other.append([2 * pair[this] + 1, 2 * pair[this]])
        order.append([0, 1] + sum(reached, []) + sum(other, []))

    tied = lax.optimization_barrier((occupied, virtual, occ_mask, virt_mask, late_given))
    pairs = basis * basis
    mix = jax.ShapeDtypeStruct((pairs, pairs), jnp.bfloat16)
    high, low = pl.pallas_call(
        functools.partial(mixing_kernel, order),
        out_shape=(mix, mix),
        in_specs=[SMEM] + [VMEM] * 4,
        out_specs=(VMEM, VMEM),
    )(jnp.stack([me, lane]), *tied[:4])
    blocks = [mine, mate] + got + [early, late]
    return pl.pallas_call(
        functools.partial(product_kernel, len(blocks)),
        out_shape=jax.ShapeDtypeStruct((aux // rows, aux), jnp.float32),
        in_specs=[SMEM] + [VMEM] * (2 + len(blocks)),
        out_specs=VMEM,
    )(lax.axis_index("row").reshape(1), high, low, *blocks)


def per_device(*given):
    integrals, occupied = given[0], given[1]
    basis, local, aux = integrals.shape
    rows, cols = lax.axis_size("row"), lax.axis_size("col")
    devices = rows * cols
    lighter = devices * integrals.size <= 2 * aux * aux
    shaped = local == 1 and cols % 2 == 0 and devices & (devices - 1) == 0 and devices >= 8
    tiled = basis % 8 == 0 and aux // rows % 128 == 0
    if lighter and shaped and tiled:
        return by_gathering(*given)
    return by_reduction(*given)


def solution(mesh):
    placed = (
        P("groups", ("row", "col"), None),
        P("groups", None),
        P("groups", None),
        P("groups", ("row", "col"), None),
        P("groups", None),
        P("groups", None),
    )
    return jax.shard_map(
        per_device,
        mesh=mesh,
        in_specs=placed,
        out_specs=P(("groups", "row"), None),
        check_vma=False,
    )
```

```python
import functools

import jax
import jax.numpy as jnp
from jax import lax
from jax.experimental import pallas as pl
from jax.experimental.pallas import tpu as pltpu
from jax.sharding import PartitionSpec as P

HIGHEST = lax.Precision.HIGHEST


def spread_two(mask, tile_rows, tile_cols):
    outer, inner = mask.shape
    wide = jnp.broadcast_to(mask[:, None, :, None], (outer, tile_rows, inner, tile_cols))
    return wide.reshape(outer * tile_rows, inner * tile_cols).astype(jnp.float32)


def spread_three(mask, tile_rows, tile_cols):
    outer, middle, inner = mask.shape
    wide = jnp.broadcast_to(mask[:, None, :, :, None], (outer, tile_rows, middle, inner, tile_cols))
    return wide.reshape(outer * tile_rows, middle, inner * tile_cols).astype(jnp.float32)


def by_reduction(integrals, occupied, virtual, int_mask, occ_mask, virt_mask):
    basis = occupied.shape[0]
    local_pairs = integrals.shape[1]
    aux_count = integrals.shape[2]
    green_tile = basis // occ_mask.shape[0]
    aux_tile = aux_count // int_mask.shape[2]
    row_count = lax.axis_size("row")
    col_count = lax.axis_size("col")
    int_full = integrals * spread_three(int_mask, green_tile, aux_tile)
    occ_full = occupied * spread_two(occ_mask, green_tile, green_tile)
    virt_full = virtual * spread_two(virt_mask, green_tile, green_tile)
    flat = int_full.reshape(basis, local_pairs * aux_count)
    contract_first = (((0,), (0,)), ((), ()))
    trans_virt = lax.dot_general(
        virt_full, flat, contract_first, precision=HIGHEST, preferred_element_type=jnp.float32
    )
    shaped_virt = trans_virt.reshape(row_count, col_count, local_pairs, local_pairs, aux_count)
    mirrored = lax.all_to_all(
        lax.all_to_all(shaped_virt, "row", split_axis=0, concat_axis=0, tiled=True),
        "col",
        split_axis=1,
        concat_axis=1,
        tiled=True,
    )
    trans_occ = lax.dot_general(
        occ_full, flat, contract_first, precision=HIGHEST, preferred_element_type=jnp.float32
    )
    shaped_occ = trans_occ.reshape(row_count, col_count, local_pairs, local_pairs, aux_count)
    pair_dims = (((0, 1, 2, 3), (0, 1, 3, 2)), ((), ()))
    whole = (
        lax.dot_general(
            shaped_occ, mirrored, pair_dims, precision=HIGHEST, preferred_element_type=jnp.float32
        )
        / basis
    )
    summed = lax.psum(whole, "col")
    return lax.psum_scatter(summed, "row", scatter_dimension=0, tiled=True)


def iota(shape, dim):
    return lax.broadcasted_iota(jnp.int32, shape, dim)


def one_hot(rows, cols, row_tile, col_tile):
    return (iota((rows, cols), 0) // row_tile == iota((rows, cols), 1) // col_tile).astype(jnp.float32)


def repeat_rows(mask, tile):
    rows = [jnp.broadcast_to(mask[i : i + 1], (tile, mask.shape[1])) for i in range(mask.shape[0])]
    return jnp.concatenate(rows, 0)


def dot(a, b, dims=((1,), (0,)), precision=HIGHEST):
    return lax.dot_general(a, b, (dims, ((), ())), precision=precision, preferred_element_type=jnp.float32)


def masking_kernel(tiles, packed, out):
    basis, aux = out.shape
    mask = packed[:-basis, 0, :]
    narrow = repeat_rows(mask[:, :tiles], basis // mask.shape[0])
    out[...] = packed[-basis:, 0, :] * dot(narrow, one_hot(tiles, aux, 1, aux // tiles), precision=None)


def split(x):
    high = x.astype(jnp.bfloat16)
    return high, (x - high.astype(jnp.float32)).astype(jnp.bfloat16)


def mixing_kernel(order, owner, occupied, virtual, occ_mask, virt_mask, high, low):
    basis = occupied.shape[0]
    tile = basis // occ_mask.shape[0]
    me, lane = owner[0], owner[1]
    picked = jnp.zeros((basis, basis), jnp.int32)
    column = iota((basis, basis), 1)
    for j in range(basis):
        lam = me ^ jnp.where(lane == 1, order[1][j], order[0][j])
        picked = jnp.where(column == j, lam, picked)
    pick = (iota((basis, basis), 0) == picked).astype(jnp.float32)
    wide = one_hot(basis // tile, basis, 1, tile)
    occ_full = occupied[...] * dot(repeat_rows(occ_mask[...].astype(jnp.float32), tile), wide)
    virt_full = virtual[...] * dot(repeat_rows(virt_mask[...].astype(jnp.float32), tile), wide)
    occ_cols = dot(occ_full, pick)
    virt_rows = dot(pick, virt_full, ((0,), (1,)))
    pairs = basis * basis
    occ_wide = dot(occ_cols, one_hot(basis, pairs, 1, basis)) * (1.0 / basis)
    cycle = (iota((basis, pairs), 0) == lax.rem(iota((basis, pairs), 1), basis)).astype(jnp.float32)
    virt_wide = dot(virt_rows, cycle)
    for j in range(basis):
        mix = occ_wide * virt_wide[j : j + 1]
        high[j * basis : (j + 1) * basis, :], low[j * basis : (j + 1) * basis, :] = split(mix)


def dot_split(a, b, dims=((1,), (0,))):
    return dot(a[0], b[0], dims, None) + (dot(a[0], b[1], dims, None) + dot(a[1], b[0], dims, None))


def product_kernel(count, *refs):
    row, high, low = refs[:3]
    blocks, out = refs[3 : 3 + count], refs[3 + count]
    rows = out.shape[0]
    start = pl.multiple_of(row[0] * rows, 128)
    own = jnp.concatenate([b[:, pl.ds(start, rows)] for b in blocks], 0)
    mixed = dot_split(split(own), (high[...], low[...]), ((0,), (0,)))
    whole = jnp.concatenate([b[...] for b in blocks], 0)
    out[...] = dot_split(split(mixed), split(whole))


VMEM = pl.BlockSpec(memory_space=pltpu.VMEM)
SMEM = pl.BlockSpec(memory_space=pltpu.SMEM)
ANY = pl.BlockSpec(memory_space=pl.ANY)
SMALL = pltpu.CompilerParams(vmem_limit_bytes=8 * 2**20)


def by_gathering(integrals, occupied, virtual, int_mask, occ_mask, virt_mask):
    basis, _, aux = integrals.shape
    axes = ("row", "col")
    rows = lax.axis_size("row")
    devices = rows * lax.axis_size("col")
    units = devices // 2
    me = lax.axis_index("row") * lax.axis_size("col") + lax.axis_index("col")
    lane = me % 2

    def exchange(block, odd, even):
        return lax.ppermute(block, axes, [(i, i ^ (odd if i % 2 else even)) for i in range(devices)])

    first = units - 1
    steps = [(2, 1)] + [(k, k + 1) for k in range(3, first, 2)]
    tiles = int_mask.shape[2]
    kept = jnp.pad(int_mask, ((0, basis), (0, 0), (0, aux - tiles)))
    wide_rows = jnp.pad(integrals, ((int_mask.shape[0], 0), (0, 0), (0, 0)))
    packed = jnp.where(lax.broadcasted_iota(jnp.int32, wide_rows.shape, 0) < int_mask.shape[0], kept.astype(jnp.float32), wide_rows)
    mine = pl.pallas_call(
        functools.partial(masking_kernel, tiles),
        out_shape=jax.ShapeDtypeStruct((basis, aux), jnp.float32),
        in_specs=[VMEM],
        out_specs=VMEM,
        compiler_params=SMALL,
    )(packed)
    both = jnp.concatenate([mine, exchange(mine, 1, 1)], 0)
    got = [exchange(mine, 2 * first, 2 * first)]
    got += [exchange(both, 2 * odd, 2 * even) for odd, even in steps]
    order = []
    for this in (0, 1):
        mine_reached = [[2 * first]]
        mates = [[2 * first + 1]]
        for pair in steps:
            mine_reached.append([2 * pair[1 - this], 2 * pair[1 - this] + 1])
            mates.append([2 * pair[this] + 1, 2 * pair[this]])
        order.append([0, 1] + sum(mine_reached, []) + sum(mates, []))

    owner, _ = lax.optimization_barrier((jnp.stack([me, lane]), both))
    pairs = basis * basis
    mix = jax.ShapeDtypeStruct((pairs, pairs), jnp.bfloat16)
    high, low = pl.pallas_call(
        functools.partial(mixing_kernel, order),
        out_shape=(mix, mix),
        in_specs=[SMEM] + [VMEM] * 4,
        out_specs=(VMEM, VMEM),
        compiler_params=SMALL,
    )(owner, occupied, virtual, occ_mask, virt_mask)
    given, high, low = lax.optimization_barrier((jnp.concatenate(got, 0), high, low))
    blocks = [both] + got + [exchange(given, 1, 1)]
    return pl.pallas_call(
        functools.partial(product_kernel, len(blocks)),
        out_shape=jax.ShapeDtypeStruct((aux // rows, aux), jnp.float32),
        in_specs=[SMEM] + [VMEM] * (2 + len(blocks)),
        out_specs=VMEM,
        compiler_params=SMALL,
    )(lax.axis_index("row").reshape(1), high, low, *blocks)


def per_device(*given):
    integrals, occupied = given[0], given[1]
    basis, local, aux = integrals.shape
    rows, cols = lax.axis_size("row"), lax.axis_size("col")
    devices = rows * cols
    lighter = devices * integrals.size <= 2 * aux * aux
    shaped = local == 1 and cols % 2 == 0 and devices & (devices - 1) == 0 and devices >= 8
    tiled = basis % 8 == 0 and aux // rows % 128 == 0
    if lighter and shaped and tiled:
        return by_gathering(*given)
    return by_reduction(*given)


def solution(mesh):
    placed = (
        P("groups", ("row", "col"), None),
        P("groups", None),
        P("groups", None),
        P("groups", ("row", "col"), None),
        P("groups", None),
        P("groups", None),
    )
    return jax.shard_map(
        per_device,
        mesh=mesh,
        in_specs=placed,
        out_specs=P(("groups", "row"), None),
        check_vma=False,
    )
```

```python
import functools

import jax
import jax.numpy as jnp
from jax import lax
from jax.experimental import pallas as pl
from jax.experimental.pallas import tpu as pltpu
from jax.sharding import PartitionSpec as P

HIGHEST = lax.Precision.HIGHEST


def spread_two(mask, tile_rows, tile_cols):
    outer, inner = mask.shape
    wide = jnp.broadcast_to(mask[:, None, :, None], (outer, tile_rows, inner, tile_cols))
    return wide.reshape(outer * tile_rows, inner * tile_cols).astype(jnp.float32)


def spread_three(mask, tile_rows, tile_cols):
    outer, middle, inner = mask.shape
    wide = jnp.broadcast_to(mask[:, None, :, :, None], (outer, tile_rows, middle, inner, tile_cols))
    return wide.reshape(outer * tile_rows, middle, inner * tile_cols).astype(jnp.float32)


def by_reduction(integrals, occupied, virtual, int_mask, occ_mask, virt_mask):
    basis = occupied.shape[0]
    local_pairs = integrals.shape[1]
    aux_count = integrals.shape[2]
    green_tile = basis // occ_mask.shape[0]
    aux_tile = aux_count // int_mask.shape[2]
    row_count = lax.axis_size("row")
    col_count = lax.axis_size("col")
    int_full = integrals * spread_three(int_mask, green_tile, aux_tile)
    occ_full = occupied * spread_two(occ_mask, green_tile, green_tile)
    virt_full = virtual * spread_two(virt_mask, green_tile, green_tile)
    flat = int_full.reshape(basis, local_pairs * aux_count)
    contract_first = (((0,), (0,)), ((), ()))
    trans_virt = lax.dot_general(
        virt_full, flat, contract_first, precision=HIGHEST, preferred_element_type=jnp.float32
    )
    shaped_virt = trans_virt.reshape(row_count, col_count, local_pairs, local_pairs, aux_count)
    mirrored = lax.all_to_all(
        lax.all_to_all(shaped_virt, "row", split_axis=0, concat_axis=0, tiled=True),
        "col",
        split_axis=1,
        concat_axis=1,
        tiled=True,
    )
    trans_occ = lax.dot_general(
        occ_full, flat, contract_first, precision=HIGHEST, preferred_element_type=jnp.float32
    )
    shaped_occ = trans_occ.reshape(row_count, col_count, local_pairs, local_pairs, aux_count)
    pair_dims = (((0, 1, 2, 3), (0, 1, 3, 2)), ((), ()))
    whole = (
        lax.dot_general(
            shaped_occ, mirrored, pair_dims, precision=HIGHEST, preferred_element_type=jnp.float32
        )
        / basis
    )
    summed = lax.psum(whole, "col")
    return lax.psum_scatter(summed, "row", scatter_dimension=0, tiled=True)


def iota(shape, dim):
    return lax.broadcasted_iota(jnp.int32, shape, dim)


def one_hot(rows, cols, row_tile, col_tile):
    return (iota((rows, cols), 0) // row_tile == iota((rows, cols), 1) // col_tile).astype(jnp.float32)


def repeat_rows(mask, tile):
    rows = [jnp.broadcast_to(mask[i : i + 1], (tile, mask.shape[1])) for i in range(mask.shape[0])]
    return jnp.concatenate(rows, 0)


def dot(a, b, dims=((1,), (0,)), precision=HIGHEST):
    return lax.dot_general(a, b, (dims, ((), ())), precision=precision, preferred_element_type=jnp.float32)


def masking_kernel(tiles, packed, out):
    basis, aux = out.shape
    mask = packed[:-basis, 0, :]
    narrow = repeat_rows(mask[:, :tiles], basis // mask.shape[0])
    out[...] = packed[-basis:, 0, :] * dot(narrow, one_hot(tiles, aux, 1, aux // tiles), precision=None)


def split(x):
    high = x.astype(jnp.bfloat16)
    return high, (x - high.astype(jnp.float32)).astype(jnp.bfloat16)


def mixing_kernel(order, owner, occupied, virtual, occ_mask, virt_mask, high, low):
    basis = occupied.shape[0]
    tile = basis // occ_mask.shape[0]
    me, lane = owner[0], owner[1]
    picked = jnp.zeros((basis, basis), jnp.int32)
    column = iota((basis, basis), 1)
    for j in range(basis):
        lam = me ^ jnp.where(lane == 1, order[1][j], order[0][j])
        picked = jnp.where(column == j, lam, picked)
    pick = (iota((basis, basis), 0) == picked).astype(jnp.float32)
    wide = one_hot(basis // tile, basis, 1, tile)
    occ_full = occupied[...] * dot(repeat_rows(occ_mask[...].astype(jnp.float32), tile), wide)
    virt_full = virtual[...] * dot(repeat_rows(virt_mask[...].astype(jnp.float32), tile), wide)
    occ_cols = dot(occ_full, pick)
    virt_rows = dot(pick, virt_full, ((0,), (1,)))
    pairs = basis * basis
    occ_wide = dot(occ_cols, one_hot(basis, pairs, 1, basis)) * (1.0 / basis)
    cycle = (iota((basis, pairs), 0) == lax.rem(iota((basis, pairs), 1), basis)).astype(jnp.float32)
    virt_wide = dot(virt_rows, cycle)
    for j in range(basis):
        mix = occ_wide * virt_wide[j : j + 1]
        high[j * basis : (j + 1) * basis, :], low[j * basis : (j + 1) * basis, :] = split(mix)


def dot_split(a, b, dims=((1,), (0,))):
    return dot(a[0], b[0], dims, None) + (dot(a[0], b[1], dims, None) + dot(a[1], b[0], dims, None))


def product_kernel(count, *refs):
    row, high, low = refs[:3]
    blocks, out = refs[3 : 3 + count], refs[3 + count]
    rows = out.shape[0]
    start = pl.multiple_of(row[0] * rows, 128)
    own = jnp.concatenate([b[:, pl.ds(start, rows)] for b in blocks], 0)
    mixed = dot_split(split(own), (high[...], low[...]), ((0,), (0,)))
    whole = jnp.concatenate([b[...] for b in blocks], 0)
    out[...] = dot_split(split(mixed), split(whole))


VMEM = pl.BlockSpec(memory_space=pltpu.VMEM)
SMEM = pl.BlockSpec(memory_space=pltpu.SMEM)
ANY = pl.BlockSpec(memory_space=pl.ANY)
SMALL = pltpu.CompilerParams(vmem_limit_bytes=8 * 2**20)


def by_gathering(integrals, occupied, virtual, int_mask, occ_mask, virt_mask):
    basis, _, aux = integrals.shape
    axes = ("row", "col")
    rows = lax.axis_size("row")
    devices = rows * lax.axis_size("col")
    units = devices // 2
    me = lax.axis_index("row") * lax.axis_size("col") + lax.axis_index("col")
    lane = me % 2

    def exchange(block, odd, even):
        return lax.ppermute(block, axes, [(i, i ^ (odd if i % 2 else even)) for i in range(devices)])

    first = units // 2
    far = sorted(range(first + 1, units), key=lambda k: k % 2)
    steps = list(zip(far, range(1, first)))
    tiles = int_mask.shape[2]
    kept = jnp.pad(int_mask, ((0, basis), (0, 0), (0, aux - tiles)))
    wide_rows = jnp.pad(integrals, ((int_mask.shape[0], 0), (0, 0), (0, 0)))
    packed = jnp.where(lax.broadcasted_iota(jnp.int32, wide_rows.shape, 0) < int_mask.shape[0], kept.astype(jnp.float32), wide_rows)
    mine = pl.pallas_call(
        functools.partial(masking_kernel, tiles),
        out_shape=jax.ShapeDtypeStruct((basis, aux), jnp.float32),
        in_specs=[VMEM],
        out_specs=VMEM,
        compiler_params=SMALL,
    )(packed)
    both = jnp.concatenate([mine, exchange(mine, 1, 1)], 0)
    got = [exchange(mine, 2 * first, 2 * first)]
    got += [exchange(both, 2 * odd, 2 * even) for odd, even in steps]
    order = []
    for this in (0, 1):
        mine_reached = [[2 * first]]
        mates = [[2 * first + 1]]
        for pair in steps:
            mine_reached.append([2 * pair[1 - this], 2 * pair[1 - this] + 1])
            mates.append([2 * pair[this] + 1, 2 * pair[this]])
        order.append([0, 1] + sum(mine_reached, []) + sum(mates, []))

    owner, _ = lax.optimization_barrier((jnp.stack([me, lane]), both))
    pairs = basis * basis
    mix = jax.ShapeDtypeStruct((pairs, pairs), jnp.bfloat16)
    high, low = pl.pallas_call(
        functools.partial(mixing_kernel, order),
        out_shape=(mix, mix),
        in_specs=[SMEM] + [VMEM] * 4,
        out_specs=(VMEM, VMEM),
        compiler_params=SMALL,
    )(owner, occupied, virtual, occ_mask, virt_mask)
    cut = len(got) // 2
    early = exchange(jnp.concatenate(got[:cut], 0), 1, 1)
    given, high, low = lax.optimization_barrier((jnp.concatenate(got[cut:], 0), high, low))
    blocks = [both] + got + [early, exchange(given, 1, 1)]
    return pl.pallas_call(
        functools.partial(product_kernel, len(blocks)),
        out_shape=jax.ShapeDtypeStruct((aux // rows, aux), jnp.float32),
        in_specs=[SMEM] + [VMEM] * (2 + len(blocks)),
        out_specs=VMEM,
        compiler_params=SMALL,
    )(lax.axis_index("row").reshape(1), high, low, *blocks)


def per_device(*given):
    integrals, occupied = given[0], given[1]
    basis, local, aux = integrals.shape
    rows, cols = lax.axis_size("row"), lax.axis_size("col")
    devices = rows * cols
    lighter = devices * integrals.size <= 2 * aux * aux
    shaped = local == 1 and cols % 2 == 0 and devices & (devices - 1) == 0 and devices >= 8
    tiled = basis % 8 == 0 and aux // rows % 128 == 0
    if lighter and shaped and tiled:
        return by_gathering(*given)
    return by_reduction(*given)


def solution(mesh):
    placed = (
        P("groups", ("row", "col"), None),
        P("groups", None),
        P("groups", None),
        P("groups", ("row", "col"), None),
        P("groups", None),
        P("groups", None),
    )
    return jax.shard_map(
        per_device,
        mesh=mesh,
        in_specs=placed,
        out_specs=P(("groups", "row"), None),
        check_vma=False,
    )
```

```python
import functools

import jax
import jax.numpy as jnp
from jax import lax
from jax.experimental import pallas as pl
from jax.experimental.pallas import tpu as pltpu
from jax.sharding import PartitionSpec as P

HIGHEST = lax.Precision.HIGHEST


def spread_two(mask, tile_rows, tile_cols):
    outer, inner = mask.shape
    wide = jnp.broadcast_to(mask[:, None, :, None], (outer, tile_rows, inner, tile_cols))
    return wide.reshape(outer * tile_rows, inner * tile_cols).astype(jnp.float32)


def spread_three(mask, tile_rows, tile_cols):
    outer, middle, inner = mask.shape
    wide = jnp.broadcast_to(mask[:, None, :, :, None], (outer, tile_rows, middle, inner, tile_cols))
    return wide.reshape(outer * tile_rows, middle, inner * tile_cols).astype(jnp.float32)


def by_reduction(integrals, occupied, virtual, int_mask, occ_mask, virt_mask):
    basis = occupied.shape[0]
    local_pairs = integrals.shape[1]
    aux_count = integrals.shape[2]
    green_tile = basis // occ_mask.shape[0]
    aux_tile = aux_count // int_mask.shape[2]
    row_count = lax.axis_size("row")
    col_count = lax.axis_size("col")
    int_full = integrals * spread_three(int_mask, green_tile, aux_tile)
    occ_full = occupied * spread_two(occ_mask, green_tile, green_tile)
    virt_full = virtual * spread_two(virt_mask, green_tile, green_tile)
    flat = int_full.reshape(basis, local_pairs * aux_count)
    contract_first = (((0,), (0,)), ((), ()))
    trans_virt = lax.dot_general(
        virt_full, flat, contract_first, precision=HIGHEST, preferred_element_type=jnp.float32
    )
    shaped_virt = trans_virt.reshape(row_count, col_count, local_pairs, local_pairs, aux_count)
    mirrored = lax.all_to_all(
        lax.all_to_all(shaped_virt, "row", split_axis=0, concat_axis=0, tiled=True),
        "col",
        split_axis=1,
        concat_axis=1,
        tiled=True,
    )
    trans_occ = lax.dot_general(
        occ_full, flat, contract_first, precision=HIGHEST, preferred_element_type=jnp.float32
    )
    shaped_occ = trans_occ.reshape(row_count, col_count, local_pairs, local_pairs, aux_count)
    pair_dims = (((0, 1, 2, 3), (0, 1, 3, 2)), ((), ()))
    whole = (
        lax.dot_general(
            shaped_occ, mirrored, pair_dims, precision=HIGHEST, preferred_element_type=jnp.float32
        )
        / basis
    )
    summed = lax.psum(whole, "col")
    return lax.psum_scatter(summed, "row", scatter_dimension=0, tiled=True)


def iota(shape, dim):
    return lax.broadcasted_iota(jnp.int32, shape, dim)


def one_hot(rows, cols, row_tile, col_tile):
    return (iota((rows, cols), 0) // row_tile == iota((rows, cols), 1) // col_tile).astype(jnp.float32)


def repeat_rows(mask, tile):
    rows = [jnp.broadcast_to(mask[i : i + 1], (tile, mask.shape[1])) for i in range(mask.shape[0])]
    return jnp.concatenate(rows, 0)


def dot(a, b, dims=((1,), (0,)), precision=HIGHEST):
    return lax.dot_general(a, b, (dims, ((), ())), precision=precision, preferred_element_type=jnp.float32)


def masking_kernel(tiles, packed, out):
    basis, aux = out.shape
    mask = packed[:-basis, 0, :]
    narrow = repeat_rows(mask[:, :tiles], basis // mask.shape[0])
    out[...] = packed[-basis:, 0, :] * dot(narrow, one_hot(tiles, aux, 1, aux // tiles), precision=None)


def split(x):
    high = x.astype(jnp.bfloat16)
    return high, (x - high.astype(jnp.float32)).astype(jnp.bfloat16)


def mixing_kernel(order, owner, occupied, virtual, occ_mask, virt_mask, high, low):
    basis = occupied.shape[0]
    tile = basis // occ_mask.shape[0]
    me, lane = owner[0], owner[1]
    picked = jnp.zeros((basis, basis), jnp.int32)
    column = iota((basis, basis), 1)
    for j in range(basis):
        lam = me ^ jnp.where(lane == 1, order[1][j], order[0][j])
        picked = jnp.where(column == j, lam, picked)
    pick = (iota((basis, basis), 0) == picked).astype(jnp.float32)
    wide = one_hot(basis // tile, basis, 1, tile)
    occ_full = occupied[...] * dot(repeat_rows(occ_mask[...].astype(jnp.float32), tile), wide)
    virt_full = virtual[...] * dot(repeat_rows(virt_mask[...].astype(jnp.float32), tile), wide)
    occ_cols = dot(occ_full, pick)
    virt_rows = dot(pick, virt_full, ((0,), (1,)))
    pairs = basis * basis
    occ_wide = dot(occ_cols, one_hot(basis, pairs, 1, basis)) * (1.0 / basis)
    cycle = (iota((basis, pairs), 0) == lax.rem(iota((basis, pairs), 1), basis)).astype(jnp.float32)
    virt_wide = dot(virt_rows, cycle)
    for j in range(basis):
        mix = occ_wide * virt_wide[j : j + 1]
        high[j * basis : (j + 1) * basis, :], low[j * basis : (j + 1) * basis, :] = split(mix)


def dot_split(a, b, dims=((1,), (0,))):
    kept = 1 - dims[0][0]
    count = a[0].shape[kept]
    tall = dot(jnp.concatenate(a, kept), b[0], dims, None)
    return tall[:count] + (tall[count:] + dot(a[0], b[1], dims, None))


def product_kernel(count, *refs):
    row, high, low = refs[:3]
    blocks, out = refs[3 : 3 + count], refs[3 + count]
    rows = out.shape[0]
    start = pl.multiple_of(row[0] * rows, 128)
    own = jnp.concatenate([b[:, pl.ds(start, rows)] for b in blocks], 0)
    mixed = dot_split(split(own), (high[...], low[...]), ((0,), (0,)))
    whole = jnp.concatenate([b[...] for b in blocks], 0)
    out[...] = dot_split(split(mixed), split(whole))


VMEM = pl.BlockSpec(memory_space=pltpu.VMEM)
SMEM = pl.BlockSpec(memory_space=pltpu.SMEM)
SMALL = pltpu.CompilerParams(vmem_limit_bytes=8 * 2**20)


def by_gathering(integrals, occupied, virtual, int_mask, occ_mask, virt_mask):
    basis, _, aux = integrals.shape
    axes = ("row", "col")
    rows = lax.axis_size("row")
    devices = rows * lax.axis_size("col")
    units = devices // 2
    me = lax.axis_index("row") * lax.axis_size("col") + lax.axis_index("col")
    lane = me % 2

    def exchange(block, odd, even):
        return lax.ppermute(block, axes, [(i, i ^ (odd if i % 2 else even)) for i in range(devices)])

    first = units // 2
    far = sorted(range(first + 1, units), key=lambda k: k % 2)
    steps = list(zip(far, range(1, first)))
    tiles = int_mask.shape[2]
    kept = jnp.pad(int_mask, ((0, basis), (0, 0), (0, aux - tiles)))
    wide_rows = jnp.pad(integrals, ((int_mask.shape[0], 0), (0, 0), (0, 0)))
    packed = jnp.where(lax.broadcasted_iota(jnp.int32, wide_rows.shape, 0) < int_mask.shape[0], kept.astype(jnp.float32), wide_rows)
    mine = pl.pallas_call(
        functools.partial(masking_kernel, tiles),
        out_shape=jax.ShapeDtypeStruct((basis, aux), jnp.float32),
        in_specs=[VMEM],
        out_specs=VMEM,
        compiler_params=SMALL,
    )(packed)
    both = jnp.concatenate([mine, exchange(mine, 1, 1)], 0)
    got = [exchange(mine, 2 * first, 2 * first)]
    got += [exchange(both, 2 * odd, 2 * even) for odd, even in steps]
    order = []
    for this in (0, 1):
        mine_reached = [[2 * first]]
        mates = [[2 * first + 1]]
        for pair in steps:
            mine_reached.append([2 * pair[1 - this], 2 * pair[1 - this] + 1])
            mates.append([2 * pair[this] + 1, 2 * pair[this]])
        order.append([0, 1] + sum(mine_reached, []) + sum(mates, []))

    owner, _ = lax.optimization_barrier((jnp.stack([me, lane]), both))
    pairs = basis * basis
    mix = jax.ShapeDtypeStruct((pairs, pairs), jnp.bfloat16)
    high, low = pl.pallas_call(
        functools.partial(mixing_kernel, order),
        out_shape=(mix, mix),
        in_specs=[SMEM] + [VMEM] * 4,
        out_specs=(VMEM, VMEM),
        compiler_params=SMALL,
    )(owner, occupied, virtual, occ_mask, virt_mask)
    cut = len(got) // 2
    early = exchange(jnp.concatenate(got[:cut], 0), 1, 1)
    given, high, low = lax.optimization_barrier((jnp.concatenate(got[cut:], 0), high, low))
    blocks = [both] + got + [early, exchange(given, 1, 1)]
    return pl.pallas_call(
        functools.partial(product_kernel, len(blocks)),
        out_shape=jax.ShapeDtypeStruct((aux // rows, aux), jnp.float32),
        in_specs=[SMEM] + [VMEM] * (2 + len(blocks)),
        out_specs=VMEM,
        compiler_params=SMALL,
    )(lax.axis_index("row").reshape(1), high, low, *blocks)


def per_device(*given):
    integrals, occupied = given[0], given[1]
    basis, local, aux = integrals.shape
    rows, cols = lax.axis_size("row"), lax.axis_size("col")
    devices = rows * cols
    lighter = devices * integrals.size <= 2 * aux * aux
    shaped = local == 1 and cols % 2 == 0 and devices & (devices - 1) == 0 and devices >= 8
    tiled = basis % 16 == 0 and aux // rows % 128 == 0
    if lighter and shaped and tiled:
        return by_gathering(*given)
    return by_reduction(*given)


def solution(mesh):
    placed = (
        P("groups", ("row", "col"), None),
        P("groups", None),
        P("groups", None),
        P("groups", ("row", "col"), None),
        P("groups", None),
        P("groups", None),
    )
    return jax.shard_map(
        per_device,
        mesh=mesh,
        in_specs=placed,
        out_specs=P(("groups", "row"), None),
        check_vma=False,
    )
```

```python
import functools

import jax
import jax.numpy as jnp
from jax import lax
from jax.experimental import pallas as pl
from jax.experimental.pallas import tpu as pltpu
from jax.sharding import PartitionSpec as P

HIGHEST = lax.Precision.HIGHEST


def spread_two(mask, tile_rows, tile_cols):
    outer, inner = mask.shape
    wide = jnp.broadcast_to(mask[:, None, :, None], (outer, tile_rows, inner, tile_cols))
    return wide.reshape(outer * tile_rows, inner * tile_cols).astype(jnp.float32)


def spread_three(mask, tile_rows, tile_cols):
    outer, middle, inner = mask.shape
    wide = jnp.broadcast_to(mask[:, None, :, :, None], (outer, tile_rows, middle, inner, tile_cols))
    return wide.reshape(outer * tile_rows, middle, inner * tile_cols).astype(jnp.float32)


def by_reduction(integrals, occupied, virtual, int_mask, occ_mask, virt_mask):
    basis = occupied.shape[0]
    local_pairs = integrals.shape[1]
    aux_count = integrals.shape[2]
    green_tile = basis // occ_mask.shape[0]
    aux_tile = aux_count // int_mask.shape[2]
    row_count = lax.axis_size("row")
    col_count = lax.axis_size("col")
    int_full = integrals * spread_three(int_mask, green_tile, aux_tile)
    occ_full = occupied * spread_two(occ_mask, green_tile, green_tile)
    virt_full = virtual * spread_two(virt_mask, green_tile, green_tile)
    flat = int_full.reshape(basis, local_pairs * aux_count)
    contract_first = (((0,), (0,)), ((), ()))
    trans_virt = lax.dot_general(
        virt_full, flat, contract_first, precision=HIGHEST, preferred_element_type=jnp.float32
    )
    shaped_virt = trans_virt.reshape(row_count, col_count, local_pairs, local_pairs, aux_count)
    mirrored = lax.all_to_all(
        lax.all_to_all(shaped_virt, "row", split_axis=0, concat_axis=0, tiled=True),
        "col",
        split_axis=1,
        concat_axis=1,
        tiled=True,
    )
    trans_occ = lax.dot_general(
        occ_full, flat, contract_first, precision=HIGHEST, preferred_element_type=jnp.float32
    )
    shaped_occ = trans_occ.reshape(row_count, col_count, local_pairs, local_pairs, aux_count)
    pair_dims = (((0, 1, 2, 3), (0, 1, 3, 2)), ((), ()))
    whole = (
        lax.dot_general(
            shaped_occ, mirrored, pair_dims, precision=HIGHEST, preferred_element_type=jnp.float32
        )
        / basis
    )
    summed = lax.psum(whole, "col")
    return lax.psum_scatter(summed, "row", scatter_dimension=0, tiled=True)


def iota(shape, dim):
    return lax.broadcasted_iota(jnp.int32, shape, dim)


def one_hot(rows, cols, row_tile, col_tile):
    return (iota((rows, cols), 0) // row_tile == iota((rows, cols), 1) // col_tile).astype(jnp.float32)


def repeat_rows(mask, tile):
    rows = [jnp.broadcast_to(mask[i : i + 1], (tile, mask.shape[1])) for i in range(mask.shape[0])]
    return jnp.concatenate(rows, 0)


def dot(a, b, dims=((1,), (0,)), precision=HIGHEST):
    return lax.dot_general(a, b, (dims, ((), ())), precision=precision, preferred_element_type=jnp.float32)


def masking_kernel(tiles, packed, out):
    basis, aux = out.shape
    mask = packed[:-basis, 0, :]
    narrow = repeat_rows(mask[:, :tiles], basis // mask.shape[0])
    out[...] = packed[-basis:, 0, :] * dot(narrow, one_hot(tiles, aux, 1, aux // tiles), precision=None)


def split(x):
    high = x.astype(jnp.bfloat16)
    return high, (x - high.astype(jnp.float32)).astype(jnp.bfloat16)


def mixing_kernel(order, owner, occupied, virtual, occ_mask, virt_mask, high, low):
    basis = occupied.shape[0]
    tile = basis // occ_mask.shape[0]
    me, lane = owner[0], owner[1]
    picked = jnp.zeros((basis, basis), jnp.int32)
    column = iota((basis, basis), 1)
    for j in range(basis):
        lam = me ^ jnp.where(lane == 1, order[1][j], order[0][j])
        picked = jnp.where(column == j, lam, picked)
    pick = (iota((basis, basis), 0) == picked).astype(jnp.float32)
    wide = one_hot(basis // tile, basis, 1, tile)
    occ_full = occupied[...] * dot(repeat_rows(occ_mask[...].astype(jnp.float32), tile), wide)
    virt_full = virtual[...] * dot(repeat_rows(virt_mask[...].astype(jnp.float32), tile), wide)
    occ_cols = dot(occ_full, pick)
    virt_rows = dot(pick, virt_full, ((0,), (1,)))
    pairs = basis * basis
    occ_wide = dot(occ_cols, one_hot(basis, pairs, 1, basis)) * (1.0 / basis)
    cycle = (iota((basis, pairs), 0) == lax.rem(iota((basis, pairs), 1), basis)).astype(jnp.float32)
    virt_wide = dot(virt_rows, cycle)
    for j in range(basis):
        mix = occ_wide * virt_wide[j : j + 1]
        high[j * basis : (j + 1) * basis, :], low[j * basis : (j + 1) * basis, :] = split(mix)


def dot_split(a, b, dims=((1,), (0,))):
    kept = 1 - dims[0][0]
    count = a[0].shape[kept]
    tall = dot(jnp.concatenate(a, kept), b[0], dims, None)
    return tall[:count] + (tall[count:] + dot(a[0], b[1], dims, None))


def product_kernel(count, *refs):
    row, high, low = refs[:3]
    blocks, out = refs[3 : 3 + count], refs[3 + count]
    rows = out.shape[0]
    start = pl.multiple_of(row[0] * rows, 128)
    own = jnp.concatenate([b[:, pl.ds(start, rows)] for b in blocks], 0)
    mixed = dot_split(split(own), (high[...], low[...]), ((0,), (0,)))
    whole = jnp.concatenate([b[...] for b in blocks], 0)
    out[...] = dot_split(split(mixed), split(whole))


VMEM = pl.BlockSpec(memory_space=pltpu.VMEM)
SMEM = pl.BlockSpec(memory_space=pltpu.SMEM)
SMALL = pltpu.CompilerParams(vmem_limit_bytes=8 * 2**20)


def by_gathering(integrals, occupied, virtual, int_mask, occ_mask, virt_mask):
    basis, _, aux = integrals.shape
    axes = ("row", "col")
    rows = lax.axis_size("row")
    devices = rows * lax.axis_size("col")
    units = devices // 2
    me = lax.axis_index("row") * lax.axis_size("col") + lax.axis_index("col")
    lane = me % 2

    def exchange(block, odd, even):
        return lax.ppermute(block, axes, [(i, i ^ (odd if i % 2 else even)) for i in range(devices)])

    first = units // 2
    far = sorted(range(first + 1, units), key=lambda k: k % 2)
    steps = list(zip(far, range(1, first)))
    tiles = int_mask.shape[2]
    kept = jnp.pad(int_mask, ((0, basis), (0, 0), (0, aux - tiles)))
    wide_rows = jnp.pad(integrals, ((int_mask.shape[0], 0), (0, 0), (0, 0)))
    packed = jnp.where(lax.broadcasted_iota(jnp.int32, wide_rows.shape, 0) < int_mask.shape[0], kept.astype(jnp.float32), wide_rows)
    mine = pl.pallas_call(
        functools.partial(masking_kernel, tiles),
        out_shape=jax.ShapeDtypeStruct((basis, aux), jnp.float32),
        in_specs=[VMEM],
        out_specs=VMEM,
        compiler_params=SMALL,
    )(packed)
    both = jnp.concatenate([mine, exchange(mine, 1, 1)], 0)
    got = [exchange(mine, 2 * first, 2 * first)]
    got += [exchange(both, 2 * odd, 2 * even) for odd, even in steps]
    order = []
    for this in (0, 1):
        mine_reached = [[2 * first]]
        mates = [[2 * first + 1]]
        for pair in steps:
            mine_reached.append([2 * pair[1 - this], 2 * pair[1 - this] + 1])
            mates.append([2 * pair[this] + 1, 2 * pair[this]])
        order.append([0, 1] + sum(mine_reached, []) + sum(mates, []))

    owner, _ = lax.optimization_barrier((jnp.stack([me, lane]), both))
    pairs = basis * basis
    mix = jax.ShapeDtypeStruct((pairs, pairs), jnp.bfloat16)
    high, low = pl.pallas_call(
        functools.partial(mixing_kernel, order),
        out_shape=(mix, mix),
        in_specs=[SMEM] + [VMEM] * 4,
        out_specs=(VMEM, VMEM),
        compiler_params=SMALL,
        cost_estimate=pl.CostEstimate(flops=4 * basis * pairs * basis, bytes_accessed=4 * pairs * pairs, transcendentals=0),
    )(owner, occupied, virtual, occ_mask, virt_mask)
    cut = len(got) // 2
    early = exchange(jnp.concatenate(got[:cut], 0), 1, 1)
    given, high, low = lax.optimization_barrier((jnp.concatenate(got[cut:], 0), high, low))
    blocks = [both] + got + [early, exchange(given, 1, 1)]
    return pl.pallas_call(
        functools.partial(product_kernel, len(blocks)),
        out_shape=jax.ShapeDtypeStruct((aux // rows, aux), jnp.float32),
        in_specs=[SMEM] + [VMEM] * (2 + len(blocks)),
        out_specs=VMEM,
        compiler_params=SMALL,
        cost_estimate=pl.CostEstimate(flops=6 * (aux // rows) * pairs * (pairs + aux), bytes_accessed=4 * pairs * (pairs + aux), transcendentals=0),
    )(lax.axis_index("row").reshape(1), high, low, *blocks)


def per_device(*given):
    integrals, occupied = given[0], given[1]
    basis, local, aux = integrals.shape
    rows, cols = lax.axis_size("row"), lax.axis_size("col")
    devices = rows * cols
    lighter = devices * integrals.size <= 2 * aux * aux
    shaped = local == 1 and cols % 2 == 0 and devices & (devices - 1) == 0 and devices >= 8
    tiled = basis % 16 == 0 and aux // rows % 128 == 0
    if lighter and shaped and tiled:
        return by_gathering(*given)
    return by_reduction(*given)


def solution(mesh):
    placed = (
        P("groups", ("row", "col"), None),
        P("groups", None),
        P("groups", None),
        P("groups", ("row", "col"), None),
        P("groups", None),
        P("groups", None),
    )
    return jax.shard_map(
        per_device,
        mesh=mesh,
        in_specs=placed,
        out_specs=P(("groups", "row"), None),
        check_vma=False,
    )
```
